32 devices in a mesh: dp: 8 (over y, x, core), expert: 4 (over z).
Axes of the slice: x: 2, y: 2, z: 4, core: 2. Of those that a mesh axis runs over, the one named last changes fastest.
Arguments:
- tokens: bfloat16 [16384, 1024], P(('dp', 'expert')), may hold values from -6 to 6
- selections: int32 [8, 4, 4, 16], P('dp', 'expert'), may hold values from 0 to 511, as said below
- router: bfloat16 [4, 1024], P('expert'), may hold values from -0.1875 to 0.1875
- w_gate: bfloat16 [4, 1024, 512], P('expert', 'dp'), may hold values from -0.1875 to 0.1875
- w_up: bfloat16 [4, 1024, 512], P('expert', 'dp'), may hold values from -0.1875 to 0.1875
- w_down: bfloat16 [4, 512, 1024], P('expert', 'dp'), may hold values from -0.25 to 0.25
- cotangent: bfloat16 [16384, 1024], P(('dp', 'expert')), may hold values from -6 to 6
Outputs:
- mixed: bfloat16 [16384, 1024], P(('dp', 'expert'))
- grad_tokens: bfloat16 [16384, 1024], P(('dp', 'expert'))
- grad_gate: float32 [4, 1024, 512], P('expert', 'dp')
- grad_up: float32 [4, 1024, 512], P('expert', 'dp')
- grad_down: float32 [4, 512, 1024], P('expert', 'dp')
- grad_router: float32 [4, 1024], P('expert')
The draws below stay inside these ranges and needn't reach their ends.
Inputs may be any that keep to these rules, and one draw needn't show every extreme that they name: `selections`: for every block of 512 tokens and every computed expert, the 16 positions are different.
All inputs are finite; a program needn't handle non-finite values.
Results may differ from the reference program's by a relative error of at most 0.0095.
Values may be sent and summed in bfloat16 or wider, within the bound.
No kernel may reach another device: no remote copies, remote signals or barrier semaphores. Data moves between devices by JAX's collectives and lax.ppermute only.
A program may use at most 64 MiB of HBM per device.

```python
import jax
import jax.numpy as jnp
from jax import lax

D = 1024
FF = 512
TOK_DEV = 512
SLOT = 16
EXPERTS_F = 4
TOKENS = 16384
N_DP = 8
N_EXPERT = 4


def draw_selections(key, part):
    key = jax.random.fold_in(key, 7)
    scores = jax.random.randint(key, (N_DP, N_EXPERT, EXPERTS_F, TOK_DEV), 0, 65536)
    scores = scores * TOK_DEV + jnp.arange(TOK_DEV, dtype=jnp.int32)
    ordering = jnp.argsort(scores, axis=-1)
    return ordering[..., :SLOT].astype(jnp.int32)


def steps_of(key, shape, pieces, least, top_value):
    def one(axis_at, shards_of):
        heights = jax.random.uniform(jax.random.fold_in(jax.random.fold_in(key, 6), axis_at), (shards_of,), jnp.float32, least / len(pieces), top_value / len(pieces))
        return jnp.repeat(jnp.exp(heights), shape[axis_at] // shards_of).reshape((-1,) + (1,) * (len(shape) - axis_at - 1))

    level = one(*pieces[0])
    for cut in pieces[1:]:
        level = level * one(*cut)
    return level


def normal_values(key, shape, scale, limit, pieces=(), kind=jnp.bfloat16):
    values = jax.random.normal(key, shape, jnp.float32) * scale
    if len(pieces) > 0:
        values = steps_of(key, shape, pieces, -0.22, 0.18) * values
    return jnp.clip(values, min=-limit, max=limit).astype(kind)


def setup_inputs(seed: int = 0) -> dict:
    seeds = jax.random.split(jax.random.key(seed), 8)
    return {
        "tokens": normal_values(seeds[0], (TOKENS, D), 1.0, 6.0, ((0, 32),)),
        "selections": draw_selections(jax.random.fold_in(seeds[7], 71), 0),
        "router": normal_values(seeds[2], (EXPERTS_F, D), D ** -0.5, 0.1875, ((0, 4),)),
        "w_gate": normal_values(seeds[3], (EXPERTS_F, D, FF), D ** -0.5, 0.1875, ((0, 4), (1, 8))),
        "w_up": normal_values(seeds[4], (EXPERTS_F, D, FF), D ** -0.5, 0.1875, ((0, 4), (1, 8))),
        "w_down": normal_values(seeds[5], (EXPERTS_F, FF, D), FF ** -0.5, 0.25, ((0, 4), (1, 8))),
        "cotangent": normal_values(seeds[6], (TOKENS, D), 1.0, 6.0, ((0, 32),)),
    }


def pick_rows(block, chosen):
    taken = jax.vmap(lambda source, index_set: source[index_set])(block, chosen)
    return taken.transpose(1, 0, 2, 3).reshape(EXPERTS_F, N_EXPERT * SLOT, D)


def place_rows(expert_rows, chosen):
    spread = expert_rows.astype(jnp.float32).reshape(EXPERTS_F, N_EXPERT, SLOT, D).transpose(1, 0, 2, 3)

    def add_source(source_rows, index_set):
        empty_rows = jnp.zeros((TOK_DEV, D), jnp.float32)
        return empty_rows.at[index_set.reshape(-1)].add(source_rows.reshape(-1, D))

    return jax.vmap(add_source)(spread, chosen).astype(jnp.bfloat16)


def expert_pass(x_rows, d_rows, router_full, gate_full, up_full, down_full):
    x_full = x_rows.astype(jnp.float32)
    logit = jnp.einsum("ecd,ed->ec", x_full, router_full)
    gate_val = jax.nn.sigmoid(logit)
    act_gate = jnp.einsum("ecd,edf->ecf", x_full, gate_full)
    act_up = jnp.einsum("ecd,edf->ecf", x_full, up_full)
    silu_gate = jax.nn.silu(act_gate)
    hidden = (silu_gate * act_up).astype(jnp.bfloat16)
    hidden_full = hidden.astype(jnp.float32)
    projected = jnp.einsum("ecf,efd->ecd", hidden_full, down_full)
    expert_out = (gate_val[..., None] * projected).astype(jnp.bfloat16)
    d_full = d_rows.astype(jnp.float32)
    gate_grad = jnp.sum(d_full * projected, axis=-1)
    logit_grad = gate_grad * gate_val * (1.0 - gate_val)
    back_out = (gate_val[..., None] * d_full).astype(jnp.bfloat16)
    back_full = back_out.astype(jnp.float32)
    hidden_grad = jnp.einsum("ecd,efd->ecf", back_full, down_full)
    sigma = jax.nn.sigmoid(act_gate)
    grad_act_gate = (hidden_grad * act_up * sigma * (1.0 + act_gate * (1.0 - sigma))).astype(jnp.bfloat16)
    grad_act_up = (hidden_grad * silu_gate).astype(jnp.bfloat16)
    gate_back = grad_act_gate.astype(jnp.float32)
    up_back = grad_act_up.astype(jnp.float32)
    row_grads = jnp.einsum("ecf,edf->ecd", gate_back, gate_full) + jnp.einsum("ecf,edf->ecd", up_back, up_full)
    row_grads = (row_grads + logit_grad[..., None] * router_full[:, None, :]).astype(jnp.bfloat16)
    part_gate = jnp.einsum("ecd,ecf->edf", x_full, gate_back).astype(jnp.bfloat16)
    part_up = jnp.einsum("ecd,ecf->edf", x_full, up_back).astype(jnp.bfloat16)
    part_down = jnp.einsum("ecf,ecd->efd", hidden_full, back_full).astype(jnp.bfloat16)
    part_router = jnp.einsum("ecd,ec->ed", x_full, logit_grad)
    return expert_out, row_grads, part_gate, part_up, part_down, part_router


def reference(tokens, selections, router, w_gate, w_up, w_down, cotangent):
    blocks = tokens.reshape(N_DP, N_EXPERT, TOK_DEV, D)
    grad_blocks = cotangent.reshape(N_DP, N_EXPERT, TOK_DEV, D)
    router_full = router.astype(jnp.float32)
    gate_full = w_gate.astype(jnp.float32)
    up_full = w_up.astype(jnp.float32)
    down_full = w_down.astype(jnp.float32)

    def group_step(carry, inputs):
        sum_gate, sum_up, sum_down, sum_router = carry
        block, grad_block, chosen = inputs
        x_rows = pick_rows(block, chosen)
        d_rows = pick_rows(grad_block, chosen)
        results = expert_pass(x_rows, d_rows, router_full, gate_full, up_full, down_full)
        expert_out, row_grads, part_gate, part_up, part_down, part_router = results
        carry = (sum_gate + part_gate.astype(jnp.float32), sum_up + part_up.astype(jnp.float32),
                 sum_down + part_down.astype(jnp.float32), sum_router + part_router)
        return carry, (place_rows(expert_out, chosen), place_rows(row_grads, chosen))

    start_carry = (jnp.zeros((EXPERTS_F, D, FF), jnp.float32), jnp.zeros((EXPERTS_F, D, FF), jnp.float32),
                   jnp.zeros((EXPERTS_F, FF, D), jnp.float32), jnp.zeros((EXPERTS_F, D), jnp.float32))
    final_carry, stacked = lax.scan(group_step, start_carry, (blocks, grad_blocks, selections))
    sum_gate, sum_up, sum_down, sum_router = final_carry
    mixed = stacked[0].reshape(TOKENS, D)
    grad_tokens = stacked[1].reshape(TOKENS, D)
    return (mixed, grad_tokens, sum_gate / N_DP, sum_up / N_DP, sum_down / N_DP, sum_router / N_DP)
```

```python
import functools

import jax
import jax.numpy as jnp
from jax import lax
from jax.experimental import pallas as pl
from jax.experimental.pallas import tpu as pltpu
from jax.sharding import PartitionSpec as P

BF16 = jnp.bfloat16
F32 = jnp.float32
VMEM = pl.BlockSpec(memory_space=pltpu.VMEM)


def dot(left, right):
    return jnp.dot(left, right, preferred_element_type=F32)


def dot_rows(left, right):
    return lax.dot_general(left, right, (((0,), (0,)), ((), ())), preferred_element_type=F32)


def dot_cols(left, right):
    return lax.dot_general(left, right, (((1,), (1,)), ((), ())), preferred_element_type=F32)


def swap(value, axis, step):
    size = lax.axis_size(axis)
    return lax.ppermute(value, axis, [(i, i ^ step) for i in range(size)])


def shape(rows, columns, kind):
    return jax.ShapeDtypeStruct((rows, columns), kind)


def call(body, out_shape, args, scratch=(), flops=0, moved=0):
    return pl.pallas_call(
        body,
        out_shape=out_shape,
        in_specs=[VMEM] * len(args),
        out_specs=jax.tree.map(lambda _: VMEM, out_shape),
        scratch_shapes=list(scratch),
        compiler_params=pltpu.CompilerParams(vmem_limit_bytes=40 << 20),
        cost_estimate=pl.CostEstimate(flops=flops, bytes_accessed=moved, transcendentals=0),
    )(*args)


def pack_weights(gate_ref, up_ref, down_ref, first_ref, second_ref):
    rows = gate_ref.shape[1]
    half = gate_ref.shape[2]
    first_ref[:rows, :] = gate_ref[0]
    second_ref[:rows, :] = up_ref[0]
    first_ref[rows:, :] = down_ref[0, :, :half]
    second_ref[rows:, :] = down_ref[0, :, half:]


def take_rows(slots, chosen_ref, tokens_ref, cotangent_ref, *refs):
    out_refs, x_ref, d_ref = refs[:-2], refs[-2], refs[-1]
    picked = lax.broadcasted_iota(jnp.int32, (chosen_ref.shape[0], tokens_ref.shape[0]), 1)
    one_hot = jnp.where(picked == chosen_ref[...], 1.0, 0.0).astype(BF16)
    x_ref[...] = dot(one_hot, tokens_ref[...]).astype(BF16)
    d_ref[...] = dot(one_hot, cotangent_ref[...]).astype(BF16)
    me = lax.axis_index("expert")
    for k, out_ref in enumerate(out_refs):
        at = pl.ds(pl.multiple_of((me ^ k) * slots, slots), slots)
        out_ref[:slots, :] = x_ref[at, :]
        out_ref[slots:, :] = d_ref[at, :]


def prepare(slots, experts, chips, block, router_ref, *refs):
    got = refs[:experts]
    x_ref, d_ref = refs[experts], refs[experts + 1]
    out_refs = refs[experts + 2 :]
    for k, ref in enumerate(got):
        x_ref[k * slots : (k + 1) * slots, :] = ref[:slots, :]
        d_ref[k * slots : (k + 1) * slots, :] = ref[slots:, :]
    gate_val = gate_of(x_ref, router_ref)
    back = (gate_val * d_ref[...].astype(F32)).astype(BF16)
    width = back.shape[1]
    mine = lax.axis_index("dp") // 2
    for k, ref in enumerate(out_refs):
        start = ((mine ^ k) * (width // chips)) // block * block
        ref[:, :width] = back
        ref[:, width:] = x_ref[:, pl.ds(pl.multiple_of(start, 128), block)]


def gate_of(x_ref, router_ref):
    logit = jnp.sum(
        x_ref[...].astype(F32) * router_ref[...].astype(F32), axis=1, keepdims=True
    )
    return jax.nn.sigmoid(logit)


def expert(slots, experts, chips, block, *refs):
    devices = 2 * chips
    x_ref, d_ref, router_ref = refs[:3]
    firsts = refs[3 : 3 + devices]
    seconds = refs[3 + devices : 3 + 2 * devices]
    outs = refs[3 + 2 * devices :]
    return_refs, late_refs = outs[:experts], outs[experts : experts + chips]
    gate_w, up_w, down_w, hidden_ref = outs[experts + chips :]
    width = x_ref.shape[1]
    half = gate_w.shape[1]
    rows = width // devices
    down_rows = half // devices
    me = lax.axis_index("dp")
    for r in range(devices):
        at = pl.ds(pl.multiple_of((me ^ r) * rows, rows), rows)
        gate_w[at, :] = firsts[r][:rows, :]
        up_w[at, :] = seconds[r][:rows, :]
        at = pl.ds(pl.multiple_of((me ^ r) * down_rows, down_rows), down_rows)
        down_w[at, :half] = firsts[r][rows:, :]
        down_w[at, half:] = seconds[r][rows:, :]
    x = x_ref[...]
    d = d_ref[...]
    gate_val = gate_of(x_ref, router_ref)
    act_gate = dot(x, gate_w[...])
    act_up = dot(x, up_w[...])
    sigma = jax.nn.sigmoid(act_gate)
    silu = act_gate * sigma
    hidden = (silu * act_up).astype(BF16)
    hidden_ref[...] = hidden
    raw = dot_cols(d, down_w[...])
    gate_grad = jnp.sum(hidden.astype(F32) * raw, axis=1, keepdims=True)
    logit_grad = gate_grad * gate_val * (1.0 - gate_val)
    hidden_grad = gate_val * raw
    grad_gate = (hidden_grad * act_up * sigma * (1.0 + act_gate * (1.0 - sigma))).astype(BF16)
    grad_up = (hidden_grad * silu).astype(BF16)
    projected = dot(hidden, down_w[...])
    out_rows = (gate_val * projected).astype(BF16)
    row_grads = dot_cols(grad_gate, gate_w[...]) + dot_cols(grad_up, up_w[...])
    row_grads = (row_grads + logit_grad * router_ref[...].astype(F32)).astype(BF16)
    for k, ref in enumerate(return_refs):
        ref[:slots, :] = out_rows[k * slots : (k + 1) * slots, :]
        ref[slots:, :] = row_grads[k * slots : (k + 1) * slots, :]
    term = jnp.sum(logit_grad * x.astype(F32), axis=0, keepdims=True)
    high = term.astype(BF16).astype(F32)
    low = term - high
    tall = x.shape[0]
    mine = me // 2
    parts = width // block
    each = tall // parts
    tail = late_refs[0].shape[0] - tall
    for k, ref in enumerate(late_refs):
        start = ((mine ^ k) * (half // chips)) // block * block
        cut = hidden_ref[:, pl.ds(pl.multiple_of(start, 128), block)].astype(F32)
        lines = jnp.concatenate([cut[i * each : (i + 1) * each, :] for i in range(parts)], axis=1)
        empty = jnp.zeros((tail - each - 2, width), F32)
        ref[:tall, :half] = grad_gate
        ref[:tall, half:] = grad_up
        ref[tall:, :] = jnp.concatenate([lines, high, low, empty], axis=0).astype(BF16)


def weight_grads(chips, block, hidden_block, *refs):
    devices = 2 * chips
    mids, lates = refs[:devices], refs[devices : 2 * devices]
    gate_ref, up_ref, down_ref, router_ref, sum_ref, down_sum_ref = refs[2 * devices :]
    width = router_ref.shape[1]
    half = gate_ref.shape[2]
    tall = mids[0].shape[0]
    scale = 1.0 / devices
    parts = width // hidden_block
    each = tall // parts
    me = lax.axis_index("dp")
    feats = jnp.concatenate([m[:, width:] for m in mids], axis=0)
    backs = jnp.concatenate([m[:, :width] for m in mids], axis=0)
    grads = jnp.concatenate([t[:tall, :] for t in lates], axis=0)
    sum_ref[...] = dot_rows(feats, grads)
    rows = gate_ref.shape[1]
    at = pl.ds(pl.multiple_of((me * rows) % block, rows), rows)
    gate_ref[0] = sum_ref[at, :half] * scale
    up_ref[0] = sum_ref[at, half:] * scale
    tails = [t[tall:, :].astype(F32) for t in lates]
    hidden = jnp.concatenate(
        [t[:each, i * hidden_block : (i + 1) * hidden_block] for t in tails for i in range(parts)],
        axis=0,
    ).astype(BF16)
    down_sum_ref[...] = dot_rows(hidden, backs)
    rows = down_ref.shape[1]
    at = pl.ds(pl.multiple_of((me * rows) % hidden_block, rows), rows)
    down_ref[0] = down_sum_ref[at, :] * scale
    total = tails[0]
    for t in tails[1:]:
        total = total + t
    router_ref[...] = (total[each : each + 1, :] + total[each + 1 : each + 2, :]) * scale


def combine(slots, chosen_ref, *refs):
    got, (mixed_ref, grad_ref, out_ref, back_ref) = refs[:-4], refs[-4:]
    me = lax.axis_index("expert")
    for k, ref in enumerate(got):
        at = pl.ds(pl.multiple_of((me ^ k) * slots, slots), slots)
        out_ref[at, :] = ref[:slots, :]
        back_ref[at, :] = ref[slots:, :]
    picked = lax.broadcasted_iota(jnp.int32, (chosen_ref.shape[0], mixed_ref.shape[0]), 1)
    one_hot = jnp.where(picked == chosen_ref[...], 1.0, 0.0).astype(BF16)
    mixed_ref[...] = dot_rows(one_hot, out_ref[...]).astype(BF16)
    grad_ref[...] = dot_rows(one_hot, back_ref[...]).astype(BF16)


def local(tokens, selections, router, w_gate, w_up, w_down, cotangent):
    devices = lax.axis_size("dp")
    experts = lax.axis_size("expert")
    chips = devices // 2
    slots = selections.shape[3]
    taken = experts * slots
    held, width = tokens.shape
    rows, half = w_gate.shape[1:]
    down_rows = w_down.shape[1]
    block = max(128, 2 * rows)
    hidden_block = max(128, 2 * down_rows)
    chosen = selections.reshape(taken, 1)

    piece = shape(rows + down_rows, half, BF16)
    first, second = call(pack_weights, (piece, piece), (w_gate, w_up, w_down))
    firsts, seconds = [None] * devices, [None] * devices
    firsts[0], seconds[0] = first, second
    for k in range(1, chips):
        firsts[2 * k] = swap(first, "dp", 2 * k)
        seconds[2 * k] = swap(second, "dp", 2 * k)
    for k in range(chips):
        firsts[2 * k + 1] = swap(firsts[2 * k], "dp", 1)
        seconds[2 * k + 1] = swap(seconds[2 * k], "dp", 1)

    sent = call(
        functools.partial(take_rows, slots),
        (shape(2 * slots, width, BF16),) * experts,
        (chosen, tokens, cotangent),
        [pltpu.VMEM((taken, width), BF16)] * 2,
    )
    got = [sent[0]] + [swap(sent[k], "expert", k) for k in range(1, experts)]
    x_rows, d_rows, *mids = call(
        functools.partial(prepare, slots, experts, chips, block),
        (shape(taken, width, BF16),) * 2 + (shape(taken, width + block, BF16),) * chips,
        (router, *got),
    )
    mids = [mids[0]] + [swap(mids[k], "dp", 2 * k) for k in range(1, chips)]
    mids = mids + [swap(m, "dp", 1) for m in mids]

    lines = taken * hidden_block // width
    late_rows = taken + -(-(lines + 2) // 16) * 16
    outs = call(
        functools.partial(expert, slots, experts, chips, hidden_block),
        (shape(2 * slots, width, BF16),) * experts + (shape(late_rows, width, BF16),) * chips,
        (x_rows, d_rows, router, *firsts, *seconds),
        [
            pltpu.VMEM((width, half), BF16),
            pltpu.VMEM((width, half), BF16),
            pltpu.VMEM((half, width), BF16),
            pltpu.VMEM((taken, half), BF16),
        ],
    )
    returned, lates = outs[:experts], outs[experts:]
    returned = [returned[0]] + [swap(returned[k], "expert", k) for k in range(1, experts)]
    mixed, grad_tokens = call(
        functools.partial(combine, slots),
        (shape(held, width, BF16),) * 2,
        (chosen, *returned),
        [pltpu.VMEM((taken, width), BF16)] * 2,
    )
    lates = [lates[0]] + [swap(lates[k], "dp", 2 * k) for k in range(1, chips)]
    lates = lates + [swap(t, "dp", 1) for t in lates]
    grad_gate, grad_up, grad_down, grad_router = call(
        functools.partial(weight_grads, chips, block, hidden_block),
        (
            jax.ShapeDtypeStruct(w_gate.shape, F32),
            jax.ShapeDtypeStruct(w_up.shape, F32),
            jax.ShapeDtypeStruct(w_down.shape, F32),
            jax.ShapeDtypeStruct(router.shape, F32),
        ),
        (*mids, *lates),
        [pltpu.VMEM((block, 2 * half), F32), pltpu.VMEM((hidden_block, width), F32)],
    )
    return mixed, grad_tokens, grad_gate, grad_up, grad_down, grad_router


def solution(mesh):
    return jax.shard_map(
        local,
        mesh=mesh,
        in_specs=(
            P(("dp", "expert"), None),
            P("dp", "expert", None, None),
            P("expert", None),
            P("expert", "dp", None),
            P("expert", "dp", None),
            P("expert", "dp", None),
            P(("dp", "expert"), None),
        ),
        out_specs=(
            P(("dp", "expert"), None),
            P(("dp", "expert"), None),
            P("expert", "dp", None),
            P("expert", "dp", None),
            P("expert", "dp", None),
            P("expert", None),
        ),
        check_vma=False,
    )
```

```python
import functools

import jax
import jax.numpy as jnp
from jax import lax
from jax.experimental import pallas as pl
from jax.experimental.pallas import tpu as pltpu
from jax.sharding import PartitionSpec as P

BF16 = jnp.bfloat16
F32 = jnp.float32
VMEM = pl.BlockSpec(memory_space=pltpu.VMEM)


def dot(left, right):
    return jnp.dot(left, right, preferred_element_type=F32)


def dot_rows(left, right):
    return lax.dot_general(left, right, (((0,), (0,)), ((), ())), preferred_element_type=F32)


def dot_cols(left, right):
    return lax.dot_general(left, right, (((1,), (1,)), ((), ())), preferred_element_type=F32)


def swap(value, axis, step):
    size = lax.axis_size(axis)
    return lax.ppermute(value, axis, [(i, i ^ step) for i in range(size)])


def after(values, *others):
    return list(lax.optimization_barrier((*values, *others))[: len(values)])


def shape(rows, columns, kind):
    return jax.ShapeDtypeStruct((rows, columns), kind)


def call(body, out_shape, args, scratch=(), flops=0, moved=0, limit=16):
    return pl.pallas_call(
        body,
        out_shape=out_shape,
        in_specs=[VMEM] * len(args),
        out_specs=jax.tree.map(lambda _: VMEM, out_shape),
        scratch_shapes=list(scratch),
        compiler_params=pltpu.CompilerParams(vmem_limit_bytes=limit << 20),
        cost_estimate=pl.CostEstimate(flops=flops, bytes_accessed=moved, transcendentals=0),
    )(*args)


def pack_weights(gate_ref, up_ref, down_ref, first_ref, second_ref):
    rows = gate_ref.shape[1]
    half = gate_ref.shape[2]
    first_ref[:rows, :] = gate_ref[0]
    second_ref[:rows, :] = up_ref[0]
    first_ref[rows:, :] = down_ref[0, :, :half]
    second_ref[rows:, :] = down_ref[0, :, half:]


def join(x_ref, d_ref, sent_ref):
    experts = sent_ref.shape[0]
    slots = x_ref.shape[0] // experts
    for e in range(experts):
        sent_ref[e, :slots, :] = x_ref[e * slots : (e + 1) * slots, :]
        sent_ref[e, slots:, :] = d_ref[e * slots : (e + 1) * slots, :]


def prepare(slots, experts, chips, block, router_ref, *refs):
    got_ref, x_ref, d_ref, *out_refs = refs
    me = lax.axis_index("expert")
    for k in range(experts):
        x_ref[k * slots : (k + 1) * slots, :] = got_ref[me ^ k, :slots, :]
        d_ref[k * slots : (k + 1) * slots, :] = got_ref[me ^ k, slots:, :]
    gate_val = gate_of(x_ref, router_ref)
    back = (gate_val * d_ref[...].astype(F32)).astype(BF16)
    width = back.shape[1]
    mine = lax.axis_index("dp") // 2
    for k, ref in enumerate(out_refs):
        start = ((mine ^ k) * (width // chips)) // block * block
        ref[:, :width] = back
        ref[:, width:] = x_ref[:, pl.ds(pl.multiple_of(start, 128), block)]


def gate_of(x_ref, router_ref):
    logit = jnp.sum(
        x_ref[...].astype(F32) * router_ref[...].astype(F32), axis=1, keepdims=True
    )
    return jax.nn.sigmoid(logit)


def expert(slots, experts, chips, block, *refs):
    devices = 2 * chips
    x_ref, d_ref, router_ref = refs[:3]
    firsts = refs[3 : 3 + devices]
    seconds = refs[3 + devices : 3 + 2 * devices]
    outs = refs[3 + 2 * devices :]
    return_refs = outs[:experts]
    late_refs = outs[experts : experts + chips]
    gate_w, up_w, down_w, hidden_ref = outs[experts + chips :]
    width = x_ref.shape[1]
    half = gate_w.shape[1]
    rows = width // devices
    down_rows = half // devices
    me = lax.axis_index("dp")
    for r in range(devices):
        at = pl.ds(pl.multiple_of((me ^ r) * rows, rows), rows)
        gate_w[at, :] = firsts[r][:rows, :]
        up_w[at, :] = seconds[r][:rows, :]
        at = pl.ds(pl.multiple_of((me ^ r) * down_rows, down_rows), down_rows)
        down_w[at, :half] = firsts[r][rows:, :]
        down_w[at, half:] = seconds[r][rows:, :]
    x = x_ref[...]
    d = d_ref[...]
    gate_val = gate_of(x_ref, router_ref)
    act_gate = dot(x, gate_w[...])
    act_up = dot(x, up_w[...])
    sigma = jax.nn.sigmoid(act_gate)
    silu = act_gate * sigma
    hidden = (silu * act_up).astype(BF16)
    hidden_ref[...] = hidden
    raw = dot_cols(d, down_w[...])
    gate_grad = jnp.sum(hidden.astype(F32) * raw, axis=1, keepdims=True)
    logit_grad = gate_grad * gate_val * (1.0 - gate_val)
    hidden_grad = gate_val * raw
    grad_gate = (hidden_grad * act_up * sigma * (1.0 + act_gate * (1.0 - sigma))).astype(BF16)
    grad_up = (hidden_grad * silu).astype(BF16)
    projected = dot(hidden, down_w[...])
    out_rows = (gate_val * projected).astype(BF16)
    row_grads = dot_cols(grad_gate, gate_w[...]) + dot_cols(grad_up, up_w[...])
    row_grads = (row_grads + logit_grad * router_ref[...].astype(F32)).astype(BF16)
    for k, ref in enumerate(return_refs):
        ref[:slots, :] = out_rows[k * slots : (k + 1) * slots, :]
        ref[slots:, :] = row_grads[k * slots : (k + 1) * slots, :]
    term = jnp.sum(logit_grad * x.astype(F32), axis=0, keepdims=True)
    high = term.astype(BF16).astype(F32)
    low = term - high
    tall = x.shape[0]
    tall = x.shape[0]
    mine = me // 2
    parts = width // block
    each = tall // parts
    tail = late_refs[0].shape[0] - tall
    for k, ref in enumerate(late_refs):
        start = ((mine ^ k) * (half // chips)) // block * block
        cut = hidden_ref[:, pl.ds(pl.multiple_of(start, 128), block)].astype(F32)
        lines = jnp.concatenate([cut[i * each : (i + 1) * each, :] for i in range(parts)], axis=1)
        empty = jnp.zeros((tail - each - 2, width), F32)
        ref[:tall, :half] = grad_gate
        ref[:tall, half:] = grad_up
        ref[tall:, :] = jnp.concatenate([lines, high, low, empty], axis=0).astype(BF16)


def weight_grads(chips, block, hidden_block, *refs):
    devices = 2 * chips
    mids, lates = refs[:devices], refs[devices : 2 * devices]
    gate_ref, up_ref, down_ref, router_ref, sum_ref, down_sum_ref = refs[2 * devices :]
    width = router_ref.shape[1]
    half = gate_ref.shape[2]
    tall = mids[0].shape[0]
    scale = 1.0 / devices
    parts = width // hidden_block
    each = tall // parts
    me = lax.axis_index("dp")
    total = None
    count = devices if devices * tall <= 1024 else chips
    for c in range(devices // count):
        mid = mids[c * count : (c + 1) * count]
        late = lates[c * count : (c + 1) * count]
        feats = jnp.concatenate([m[:, width:] for m in mid], axis=0)
        backs = jnp.concatenate([m[:, :width] for m in mid], axis=0)
        grads = jnp.concatenate([t[:tall, :] for t in late], axis=0)
        term = dot_rows(feats, grads)
        sum_ref[...] = term if c == 0 else sum_ref[...] + term
        tails = [t[tall:, :].astype(F32) for t in late]
        hidden = jnp.concatenate(
            [
                t[:each, i * hidden_block : (i + 1) * hidden_block]
                for t in tails
                for i in range(parts)
            ],
            axis=0,
        ).astype(BF16)
        term = dot_rows(hidden, backs)
        down_sum_ref[...] = term if c == 0 else down_sum_ref[...] + term
        for t in tails:
            total = t if total is None else total + t
    rows = gate_ref.shape[1]
    at = pl.ds(pl.multiple_of((me * rows) % block, rows), rows)
    gate_ref[0] = sum_ref[at, :half] * scale
    up_ref[0] = sum_ref[at, half:] * scale
    rows = down_ref.shape[1]
    at = pl.ds(pl.multiple_of((me * rows) % hidden_block, rows), rows)
    down_ref[0] = down_sum_ref[at, :] * scale
    router_ref[...] = (total[each : each + 1, :] + total[each + 1 : each + 2, :]) * scale


def combine(slots, chosen_ref, *refs):
    got, (mixed_ref, grad_ref, out_ref, back_ref) = refs[:-4], refs[-4:]
    me = lax.axis_index("expert")
    for k, ref in enumerate(got):
        at = pl.ds(pl.multiple_of((me ^ k) * slots, slots), slots)
        out_ref[at, :] = ref[:slots, :]
        back_ref[at, :] = ref[slots:, :]
    chosen = chosen_ref[...]
    line = jnp.concatenate([chosen[e : e + 1, :] for e in range(len(got))], axis=1)
    picked = lax.broadcasted_iota(jnp.int32, (mixed_ref.shape[0], line.shape[1]), 0)
    one_hot = jnp.where(picked == line, 1.0, 0.0).astype(BF16)
    mixed_ref[...] = dot(one_hot, out_ref[...]).astype(BF16)
    grad_ref[...] = dot(one_hot, back_ref[...]).astype(BF16)


def local(tokens, selections, router, w_gate, w_up, w_down, cotangent):
    devices = lax.axis_size("dp")
    experts = lax.axis_size("expert")
    chips = devices // 2
    slots = selections.shape[3]
    taken = experts * slots
    held, width = tokens.shape
    rows, half = w_gate.shape[1:]
    down_rows = w_down.shape[1]
    block = max(128, 2 * rows)
    hidden_block = max(128, 2 * down_rows)

    flat = selections.reshape(taken)
    x_sent = tokens.at[flat].get(mode="promise_in_bounds")
    d_sent = cotangent.at[flat].get(mode="promise_in_bounds")
    held_weights = lax.optimization_barrier((w_gate, w_up, w_down, x_sent, d_sent))
    x_sent, d_sent = held_weights[3:]
    piece = shape(rows + down_rows, half, BF16)
    first, second = call(pack_weights, (piece, piece), held_weights[:3])
    firsts, seconds = [None] * devices, [None] * devices
    firsts[0], seconds[0] = first, second
    if chips == 4:
        firsts[2] = swap(first, "dp", 2)
        seconds[4] = swap(second, "dp", 4)
        firsts[4] = swap(first, "dp", 4)
        seconds[2] = swap(second, "dp", 2)
        firsts[6] = swap(firsts[2], "dp", 4)
        seconds[6] = swap(seconds[4], "dp", 2)
    else:
        for k in range(1, chips):
            firsts[2 * k] = swap(first, "dp", 2 * k)
            seconds[2 * k] = swap(second, "dp", 2 * k)
    for k in range(chips):
        firsts[2 * k + 1] = swap(firsts[2 * k], "dp", 1)
        seconds[2 * k + 1] = swap(seconds[2 * k], "dp", 1)

    sent = call(
        join,
        jax.ShapeDtypeStruct((experts, 2 * slots, width), BF16),
        (x_sent, d_sent),
    )
    got = [lax.all_to_all(sent, "expert", 0, 0, tiled=True)]
    got = after(got, firsts[3], firsts[5], firsts[6], seconds[3], seconds[5], seconds[6])
    x_rows, d_rows, *mids = call(
        functools.partial(prepare, slots, experts, chips, block),
        (shape(taken, width, BF16),) * 2 + (shape(taken, width + block, BF16),) * chips,
        (router, *got),
    )
    mids = [mids[0]] + [swap(mids[k], "dp", 2 * k) for k in range(1, chips)]

    lines = taken * hidden_block // width
    late_rows = taken + -(-(lines + 2) // 16) * 16
    outs = call(
        functools.partial(expert, slots, experts, chips, hidden_block),
        (shape(2 * slots, width, BF16),) * experts + (shape(late_rows, width, BF16),) * chips,
        (x_rows, d_rows, router, *firsts, *seconds),
        [
            pltpu.VMEM((width, half), BF16),
            pltpu.VMEM((width, half), BF16),
            pltpu.VMEM((half, width), BF16),
            pltpu.VMEM((taken, half), BF16),
        ],
        limit=16 if taken <= 64 else 40,
    )
    returned, lates = list(outs[:experts]), list(outs[experts:])
    own_late = lates[0]
    returned = [returned[0]] + [swap(returned[k], "expert", k) for k in range(1, experts)]
    mixed, grad_tokens = call(
        functools.partial(combine, slots),
        (shape(held, width, BF16),) * 2,
        (selections[0, 0], *returned),
        [pltpu.VMEM((taken, width), BF16)] * 2,
    )
    lates = [lates[0]] + [swap(lates[k], "dp", 2 * k) for k in range(1, chips)]
    mids = after(mids, own_late)
    mids = mids + [swap(m, "dp", 1) for m in mids]
    lates = lates + [swap(t, "dp", 1) for t in lates]
    grad_gate, grad_up, grad_down, grad_router = call(
        functools.partial(weight_grads, chips, block, hidden_block),
        (
            jax.ShapeDtypeStruct(w_gate.shape, F32),
            jax.ShapeDtypeStruct(w_up.shape, F32),
            jax.ShapeDtypeStruct(w_down.shape, F32),
            jax.ShapeDtypeStruct(router.shape, F32),
        ),
        (*mids, *lates),
        [pltpu.VMEM((block, 2 * half), F32), pltpu.VMEM((hidden_block, width), F32)],
        limit=16 if taken <= 64 else 40,
    )
    return mixed, grad_tokens, grad_gate, grad_up, grad_down, grad_router


def solution(mesh):
    return jax.shard_map(
        local,
        mesh=mesh,
        in_specs=(
            P(("dp", "expert"), None),
            P("dp", "expert", None, None),
            P("expert", None),
            P("expert", "dp", None),
            P("expert", "dp", None),
            P("expert", "dp", None),
            P(("dp", "expert"), None),
        ),
        out_specs=(
            P(("dp", "expert"), None),
            P(("dp", "expert"), None),
            P("expert", "dp", None),
            P("expert", "dp", None),
            P("expert", "dp", None),
            P("expert", None),
        ),
        check_vma=False,
    )
```

```python
import functools

import jax
import jax.numpy as jnp
from jax import lax
from jax.experimental import pallas as pl
from jax.experimental.pallas import tpu as pltpu
from jax.sharding import PartitionSpec as P

BF16 = jnp.bfloat16
F32 = jnp.float32
VMEM = pl.BlockSpec(memory_space=pltpu.VMEM)


def dot(left, right):
    return jnp.dot(left, right, preferred_element_type=F32)


def dot_rows(left, right):
    return lax.dot_general(left, right, (((0,), (0,)), ((), ())), preferred_element_type=F32)


def dot_cols(left, right):
    return lax.dot_general(left, right, (((1,), (1,)), ((), ())), preferred_element_type=F32)


def swap(value, axis, step):
    size = lax.axis_size(axis)
    return lax.ppermute(value, axis, [(i, i ^ step) for i in range(size)])


def after(values, *others):
    return list(lax.optimization_barrier((*values, *others))[: len(values)])


def shape(rows, columns, kind):
    return jax.ShapeDtypeStruct((rows, columns), kind)


def call(body, out_shape, args, scratch=(), flops=0, moved=0, limit=16):
    return pl.pallas_call(
        body,
        out_shape=out_shape,
        in_specs=[VMEM] * len(args),
        out_specs=jax.tree.map(lambda _: VMEM, out_shape),
        scratch_shapes=list(scratch),
        compiler_params=pltpu.CompilerParams(vmem_limit_bytes=limit << 20),
        cost_estimate=pl.CostEstimate(flops=flops, bytes_accessed=moved, transcendentals=0),
    )(*args)


def pack_weights(gate_ref, up_ref, down_ref, out_ref):
    rows, half = gate_ref.shape[1:]
    out_ref[:rows, :half] = gate_ref[0]
    out_ref[:rows, half:] = up_ref[0]
    out_ref[rows:, :] = down_ref[0]


def join(x_ref, d_ref, sent_ref):
    experts = sent_ref.shape[0]
    slots = x_ref.shape[0] // experts
    for e in range(experts):
        sent_ref[e, :slots, :] = x_ref[e * slots : (e + 1) * slots, :]
        sent_ref[e, slots:, :] = d_ref[e * slots : (e + 1) * slots, :]


def prepare(slots, experts, chips, block, router_ref, *refs):
    got_ref, x_ref, d_ref, *out_refs = refs
    me = lax.axis_index("expert")
    for k in range(experts):
        x_ref[k * slots : (k + 1) * slots, :] = got_ref[me ^ k, :slots, :]
        d_ref[k * slots : (k + 1) * slots, :] = got_ref[me ^ k, slots:, :]
    gate_val = gate_of(x_ref, router_ref)
    back = (gate_val * d_ref[...].astype(F32)).astype(BF16)
    width = back.shape[1]
    mine = lax.axis_index("dp") // 2
    for k, ref in enumerate(out_refs):
        start = ((mine ^ k) * (width // chips)) // block * block
        ref[:, :width] = back
        ref[:, width:] = x_ref[:, pl.ds(pl.multiple_of(start, 128), block)]


def gate_of(x_ref, router_ref):
    logit = jnp.sum(
        x_ref[...].astype(F32) * router_ref[...].astype(F32), axis=1, keepdims=True
    )
    return jax.nn.sigmoid(logit)


def hidden_part(slots, experts, chips, block, *refs):
    devices = 2 * chips
    x_ref, d_ref, router_ref = refs[:3]
    parts = refs[3 : 3 + devices]
    outs = refs[3 + devices :]
    late_refs = outs[:chips]
    hidden_ref, logit_ref, gate_w, up_w, down_w = outs[chips:]
    width = x_ref.shape[1]
    half = gate_w.shape[1]
    rows = width // devices
    down_rows = half // devices
    me = lax.axis_index("dp")
    for r in range(devices):
        at = pl.ds(pl.multiple_of((me ^ r) * rows, rows), rows)
        gate_w[at, :] = parts[r][:rows, :half]
        up_w[at, :] = parts[r][:rows, half:]
        at = pl.ds(pl.multiple_of((me ^ r) * down_rows, down_rows), down_rows)
        down_w[at, :] = parts[r][rows:, :]
    x = x_ref[...]
    d = d_ref[...]
    gate_val = gate_of(x_ref, router_ref)
    act_gate = dot(x, gate_w[...])
    act_up = dot(x, up_w[...])
    sigma = jax.nn.sigmoid(act_gate)
    silu = act_gate * sigma
    hidden = (silu * act_up).astype(BF16)
    hidden_ref[...] = hidden
    raw = dot_cols(d, down_w[...])
    gate_grad = jnp.sum(hidden.astype(F32) * raw, axis=1, keepdims=True)
    logit_grad = gate_grad * gate_val * (1.0 - gate_val)
    hidden_grad = gate_val * raw
    grad_gate = (hidden_grad * act_up * sigma * (1.0 + act_gate * (1.0 - sigma))).astype(BF16)
    grad_up = (hidden_grad * silu).astype(BF16)
    logit_ref[...] = jnp.broadcast_to(logit_grad, logit_ref.shape)
    term = jnp.sum(logit_grad * x.astype(F32), axis=0, keepdims=True)
    high = term.astype(BF16).astype(F32)
    low = term - high
    tall = x.shape[0]
    tall = x.shape[0]
    mine = me // 2
    parts = width // block
    each = tall // parts
    tail = late_refs[0].shape[0] - tall
    for k, ref in enumerate(late_refs):
        start = ((mine ^ k) * (half // chips)) // block * block
        cut = hidden_ref[:, pl.ds(pl.multiple_of(start, 128), block)].astype(F32)
        lines = jnp.concatenate([cut[i * each : (i + 1) * each, :] for i in range(parts)], axis=1)
        empty = jnp.zeros((tail - each - 2, width), F32)
        ref[:tall, :half] = grad_gate
        ref[:tall, half:] = grad_up
        ref[tall:, :] = jnp.concatenate([lines, high, low, empty], axis=0).astype(BF16)


def row_part(slots, x_ref, router_ref, late_ref, hidden_ref, logit_ref, gate_w, up_w, down_w, *outs):
    tall = x_ref.shape[0]
    half = gate_w.shape[1]
    gate_val = gate_of(x_ref, router_ref)
    out_rows = (gate_val * dot(hidden_ref[...], down_w[...])).astype(BF16)
    row_grads = dot_cols(late_ref[:tall, :half], gate_w[...])
    row_grads = row_grads + dot_cols(late_ref[:tall, half:], up_w[...])
    row_grads = (row_grads + logit_ref[:, :1] * router_ref[...].astype(F32)).astype(BF16)
    for k, ref in enumerate(outs):
        ref[:slots, :] = out_rows[k * slots : (k + 1) * slots, :]
        ref[slots:, :] = row_grads[k * slots : (k + 1) * slots, :]


def weight_grads(chips, block, hidden_block, *refs):
    devices = 2 * chips
    mids, lates = refs[:devices], refs[devices : 2 * devices]
    gate_ref, up_ref, down_ref, router_ref, sum_ref, down_sum_ref = refs[2 * devices :]
    width = router_ref.shape[1]
    half = gate_ref.shape[2]
    tall = mids[0].shape[0]
    scale = 1.0 / devices
    parts = width // hidden_block
    each = tall // parts
    me = lax.axis_index("dp")
    total = None
    count = devices if devices * tall <= 1024 else chips
    for c in range(devices // count):
        mid = mids[c * count : (c + 1) * count]
        late = lates[c * count : (c + 1) * count]
        feats = jnp.concatenate([m[:, width:] for m in mid], axis=0)
        backs = jnp.concatenate([m[:, :width] for m in mid], axis=0)
        grads = jnp.concatenate([t[:tall, :] for t in late], axis=0)
        term = dot_rows(feats, grads)
        sum_ref[...] = term if c == 0 else sum_ref[...] + term
        tails = [t[tall:, :].astype(F32) for t in late]
        hidden = jnp.concatenate(
            [
                t[:each, i * hidden_block : (i + 1) * hidden_block]
                for t in tails
                for i in range(parts)
            ],
            axis=0,
        ).astype(BF16)
        term = dot_rows(hidden, backs)
        down_sum_ref[...] = term if c == 0 else down_sum_ref[...] + term
        for t in tails:
            total = t if total is None else total + t
    rows = gate_ref.shape[1]
    at = pl.ds(pl.multiple_of((me * rows) % block, rows), rows)
    gate_ref[0] = sum_ref[at, :half] * scale
    up_ref[0] = sum_ref[at, half:] * scale
    rows = down_ref.shape[1]
    at = pl.ds(pl.multiple_of((me * rows) % hidden_block, rows), rows)
    down_ref[0] = down_sum_ref[at, :] * scale
    router_ref[...] = (total[each : each + 1, :] + total[each + 1 : each + 2, :]) * scale


def combine(slots, chosen_ref, *refs):
    got, (mixed_ref, grad_ref, out_ref, back_ref) = refs[:-4], refs[-4:]
    me = lax.axis_index("expert")
    for k, ref in enumerate(got):
        at = pl.ds(pl.multiple_of((me ^ k) * slots, slots), slots)
        out_ref[at, :] = ref[:slots, :]
        back_ref[at, :] = ref[slots:, :]
    chosen = chosen_ref[...]
    line = jnp.concatenate([chosen[e : e + 1, :] for e in range(len(got))], axis=1)
    picked = lax.broadcasted_iota(jnp.int32, (mixed_ref.shape[0], line.shape[1]), 0)
    one_hot = jnp.where(picked == line, 1.0, 0.0).astype(BF16)
    mixed_ref[...] = dot(one_hot, out_ref[...]).astype(BF16)
    grad_ref[...] = dot(one_hot, back_ref[...]).astype(BF16)


def local(tokens, selections, router, w_gate, w_up, w_down, cotangent):
    devices = lax.axis_size("dp")
    experts = lax.axis_size("expert")
    chips = devices // 2
    slots = selections.shape[3]
    taken = experts * slots
    held, width = tokens.shape
    rows, half = w_gate.shape[1:]
    down_rows = w_down.shape[1]
    block = max(128, 2 * rows)
    hidden_block = max(128, 2 * down_rows)

    flat = selections.reshape(taken)
    x_sent = tokens.at[flat].get(mode="promise_in_bounds")
    d_sent = cotangent.at[flat].get(mode="promise_in_bounds")
    held_weights = lax.optimization_barrier((w_gate, w_up, w_down, x_sent))
    x_sent = held_weights[3]
    held_part = call(pack_weights, shape(rows + down_rows, width, BF16), held_weights[:3])
    parts = [None] * devices
    parts[0] = held_part
    for k in range(1, chips):
        parts[2 * k] = swap(held_part, "dp", 2 * k)
    for k in range(chips):
        parts[2 * k + 1] = swap(parts[2 * k], "dp", 1)

    sent = call(
        join,
        jax.ShapeDtypeStruct((experts, 2 * slots, width), BF16),
        (x_sent, d_sent),
    )
    got = [lax.all_to_all(sent, "expert", 0, 0, tiled=True)]
    x_rows, d_rows, *mids = call(
        functools.partial(prepare, slots, experts, chips, block),
        (shape(taken, width, BF16),) * 2 + (shape(taken, width + block, BF16),) * chips,
        (router, *got),
    )
    mids = [mids[0]] + [swap(mids[k], "dp", 2 * k) for k in range(1, chips)]

    lines = taken * hidden_block // width
    late_rows = taken + -(-(lines + 2) // 16) * 16
    outs = call(
        functools.partial(hidden_part, slots, experts, chips, hidden_block),
        (shape(late_rows, width, BF16),) * chips
        + (
            shape(taken, half, BF16),
            shape(taken, 128, F32),
            shape(width, half, BF16),
            shape(width, half, BF16),
            shape(half, width, BF16),
        ),
        (x_rows, d_rows, router, *parts),
        limit=16 if taken <= 64 else 40,
    )
    lates = list(outs[:chips])
    returned = call(
        functools.partial(row_part, slots),
        (shape(2 * slots, width, BF16),) * experts,
        (x_rows, router, lates[0], *outs[chips:]),
        limit=16 if taken <= 64 else 40,
    )
    own_late = lates[0]
    returned = [returned[0]] + [swap(returned[k], "expert", k) for k in range(1, experts)]
    mixed, grad_tokens = call(
        functools.partial(combine, slots),
        (shape(held, width, BF16),) * 2,
        (selections[0, 0], *returned),
        [pltpu.VMEM((taken, width), BF16)] * 2,
    )
    lates = [lates[0]] + [swap(lates[k], "dp", 2 * k) for k in range(1, chips)]
    mids = after(mids, returned[1])
    mids = mids + [swap(m, "dp", 1) for m in mids]
    near = after(lates[:-1], *returned)
    far = after(lates[-1:], mixed)
    lates = lates + [swap(t, "dp", 1) for t in near + far]
    grad_gate, grad_up, grad_down, grad_router = call(
        functools.partial(weight_grads, chips, block, hidden_block),
        (
            jax.ShapeDtypeStruct(w_gate.shape, F32),
            jax.ShapeDtypeStruct(w_up.shape, F32),
            jax.ShapeDtypeStruct(w_down.shape, F32),
            jax.ShapeDtypeStruct(router.shape, F32),
        ),
        (*mids, *lates),
        [pltpu.VMEM((block, 2 * half), F32), pltpu.VMEM((hidden_block, width), F32)],
        limit=16 if taken <= 64 else 40,
    )
    return mixed, grad_tokens, grad_gate, grad_up, grad_down, grad_router


def solution(mesh):
    return jax.shard_map(
        local,
        mesh=mesh,
        in_specs=(
            P(("dp", "expert"), None),
            P("dp", "expert", None, None),
            P("expert", None),
            P("expert", "dp", None),
            P("expert", "dp", None),
            P("expert", "dp", None),
            P(("dp", "expert"), None),
        ),
        out_specs=(
            P(("dp", "expert"), None),
            P(("dp", "expert"), None),
            P("expert", "dp", None),
            P("expert", "dp", None),
            P("expert", "dp", None),
            P("expert", None),
        ),
        check_vma=False,
    )
```

```python
import functools

import jax
import jax.numpy as jnp
from jax import lax
from jax.experimental import pallas as pl
from jax.experimental.pallas import tpu as pltpu
from jax.sharding import PartitionSpec as P

BF16 = jnp.bfloat16
F32 = jnp.float32
VMEM = pl.BlockSpec(memory_space=pltpu.VMEM)


def dot(left, right):
    return jnp.dot(left, right, preferred_element_type=F32)


def dot_rows(left, right):
    return lax.dot_general(left, right, (((0,), (0,)), ((), ())), preferred_element_type=F32)


def dot_cols(left, right):
    return lax.dot_general(left, right, (((1,), (1,)), ((), ())), preferred_element_type=F32)


def swap(value, axis, step):
    size = lax.axis_size(axis)
    return lax.ppermute(value, axis, [(i, i ^ step) for i in range(size)])


def after(values, *others):
    return list(lax.optimization_barrier((*values, *others))[: len(values)])


def shape(rows, columns, kind):
    return jax.ShapeDtypeStruct((rows, columns), kind)


def call(body, out_shape, args, scratch=(), flops=0, moved=0, limit=16):
    return pl.pallas_call(
        body,
        out_shape=out_shape,
        in_specs=[VMEM] * len(args),
        out_specs=jax.tree.map(lambda _: VMEM, out_shape),
        scratch_shapes=list(scratch),
        compiler_params=pltpu.CompilerParams(vmem_limit_bytes=limit << 20),
        cost_estimate=pl.CostEstimate(flops=flops, bytes_accessed=moved, transcendentals=0),
    )(*args)


def pack_weights(gate_ref, up_ref, down_ref, out_ref):
    rows, half = gate_ref.shape[1:]
    out_ref[:rows, :half] = gate_ref[0]
    out_ref[:rows, half:] = up_ref[0]
    out_ref[rows:, :] = down_ref[0]


def join(x_ref, d_ref, sent_ref):
    experts = sent_ref.shape[0]
    slots = x_ref.shape[0] // experts
    for e in range(experts):
        sent_ref[e, :slots, :] = x_ref[e * slots : (e + 1) * slots, :]
        sent_ref[e, slots:, :] = d_ref[e * slots : (e + 1) * slots, :]


def prepare(slots, experts, chips, block, router_ref, *refs):
    got_ref, x_ref, d_ref, *out_refs = refs
    me = lax.axis_index("expert")
    for k in range(experts):
        x_ref[k * slots : (k + 1) * slots, :] = got_ref[me ^ k, :slots, :]
        d_ref[k * slots : (k + 1) * slots, :] = got_ref[me ^ k, slots:, :]
    gate_val = gate_of(x_ref, router_ref)
    back = (gate_val * d_ref[...].astype(F32)).astype(BF16)
    width = back.shape[1]
    mine = lax.axis_index("dp") // 2
    for k, ref in enumerate(out_refs):
        start = ((mine ^ k) * (width // chips)) // block * block
        ref[:, :width] = back
        ref[:, width:] = x_ref[:, pl.ds(pl.multiple_of(start, 128), block)]


def gate_of(x_ref, router_ref):
    logit = jnp.sum(
        x_ref[...].astype(F32) * router_ref[...].astype(F32), axis=1, keepdims=True
    )
    return jax.nn.sigmoid(logit)


def hidden_part(slots, experts, chips, block, *refs):
    devices = 2 * chips
    x_ref, d_ref, router_ref = refs[:3]
    parts = refs[3 : 3 + devices]
    outs = refs[3 + devices :]
    late_refs = outs[:chips]
    hidden_ref, logit_ref, gate_w, up_w, down_w = outs[chips:]
    width = x_ref.shape[1]
    half = gate_w.shape[1]
    rows = width // devices
    down_rows = half // devices
    me = lax.axis_index("dp")
    for r in range(devices):
        at = pl.ds(pl.multiple_of((me ^ r) * rows, rows), rows)
        gate_w[at, :] = parts[r][:rows, :half]
        up_w[at, :] = parts[r][:rows, half:]
        at = pl.ds(pl.multiple_of((me ^ r) * down_rows, down_rows), down_rows)
        down_w[at, :] = parts[r][rows:, :]
    x = x_ref[...]
    d = d_ref[...]
    gate_val = gate_of(x_ref, router_ref)
    act_gate = dot(x, gate_w[...])
    act_up = dot(x, up_w[...])
    sigma = jax.nn.sigmoid(act_gate)
    silu = act_gate * sigma
    hidden = (silu * act_up).astype(BF16)
    hidden_ref[...] = hidden
    raw = dot_cols(d, down_w[...])
    gate_grad = jnp.sum(hidden.astype(F32) * raw, axis=1, keepdims=True)
    logit_grad = gate_grad * gate_val * (1.0 - gate_val)
    hidden_grad = gate_val * raw
    grad_gate = (hidden_grad * act_up * sigma * (1.0 + act_gate * (1.0 - sigma))).astype(BF16)
    grad_up = (hidden_grad * silu).astype(BF16)
    logit_ref[...] = jnp.broadcast_to(logit_grad, logit_ref.shape)
    term = jnp.sum(logit_grad * x.astype(F32), axis=0, keepdims=True)
    high = term.astype(BF16).astype(F32)
    low = term - high
    tall = x.shape[0]
    tall = x.shape[0]
    mine = me // 2
    parts = width // block
    each = tall // parts
    tail = late_refs[0].shape[0] - tall
    for k, ref in enumerate(late_refs):
        start = ((mine ^ k) * (half // chips)) // block * block
        cut = hidden_ref[:, pl.ds(pl.multiple_of(start, 128), block)].astype(F32)
        lines = jnp.concatenate([cut[i * each : (i + 1) * each, :] for i in range(parts)], axis=1)
        empty = jnp.zeros((tail - each - 2, width), F32)
        ref[:tall, :half] = grad_gate
        ref[:tall, half:] = grad_up
        ref[tall:, :] = jnp.concatenate([lines, high, low, empty], axis=0).astype(BF16)


def row_part(slots, x_ref, router_ref, late_ref, hidden_ref, logit_ref, gate_w, up_w, down_w, *outs):
    tall = x_ref.shape[0]
    half = gate_w.shape[1]
    gate_val = gate_of(x_ref, router_ref)
    out_rows = (gate_val * dot(hidden_ref[...], down_w[...])).astype(BF16)
    row_grads = dot_cols(late_ref[:tall, :half], gate_w[...])
    row_grads = row_grads + dot_cols(late_ref[:tall, half:], up_w[...])
    row_grads = (row_grads + logit_ref[:, :1] * router_ref[...].astype(F32)).astype(BF16)
    for k, ref in enumerate(outs):
        ref[:slots, :] = out_rows[k * slots : (k + 1) * slots, :]
        ref[slots:, :] = row_grads[k * slots : (k + 1) * slots, :]


def weight_grads(chips, block, hidden_block, *refs):
    devices = 2 * chips
    mids, lates = refs[:devices], refs[devices : 2 * devices]
    gate_ref, up_ref, down_ref, router_ref, sum_ref, down_sum_ref = refs[2 * devices :]
    width = router_ref.shape[1]
    half = gate_ref.shape[2]
    tall = mids[0].shape[0]
    scale = 1.0 / devices
    parts = width // hidden_block
    each = tall // parts
    me = lax.axis_index("dp")
    total = None
    count = devices if devices * tall <= 1024 else chips
    for c in range(devices // count):
        mid = mids[c * count : (c + 1) * count]
        late = lates[c * count : (c + 1) * count]
        feats = jnp.concatenate([m[:, width:] for m in mid], axis=0)
        backs = jnp.concatenate([m[:, :width] for m in mid], axis=0)
        grads = jnp.concatenate([t[:tall, :] for t in late], axis=0)
        term = dot_rows(feats, grads)
        sum_ref[...] = term if c == 0 else sum_ref[...] + term
        tails = [t[tall:, :].astype(F32) for t in late]
        hidden = jnp.concatenate(
            [
                t[:each, i * hidden_block : (i + 1) * hidden_block]
                for t in tails
                for i in range(parts)
            ],
            axis=0,
        ).astype(BF16)
        term = dot_rows(hidden, backs)
        down_sum_ref[...] = term if c == 0 else down_sum_ref[...] + term
        for t in tails:
            total = t if total is None else total + t
    rows = gate_ref.shape[1]
    at = pl.ds(pl.multiple_of((me * rows) % block, rows), rows)
    gate_ref[0] = sum_ref[at, :half] * scale
    up_ref[0] = sum_ref[at, half:] * scale
    rows = down_ref.shape[1]
    at = pl.ds(pl.multiple_of((me * rows) % hidden_block, rows), rows)
    down_ref[0] = down_sum_ref[at, :] * scale
    router_ref[...] = (total[each : each + 1, :] + total[each + 1 : each + 2, :]) * scale


def combine(slots, chosen_ref, *refs):
    got, (mixed_ref, grad_ref, out_ref, back_ref) = refs[:-4], refs[-4:]
    me = lax.axis_index("expert")
    for k, ref in enumerate(got[::-1]):
        at = pl.ds(pl.multiple_of((me ^ k) * slots, slots), slots)
        out_ref[at, :] = ref[:slots, :]
        back_ref[at, :] = ref[slots:, :]
    chosen = chosen_ref[...]
    line = jnp.concatenate([chosen[e : e + 1, :] for e in range(len(got))], axis=1)
    picked = lax.broadcasted_iota(jnp.int32, (mixed_ref.shape[0], line.shape[1]), 0)
    one_hot = jnp.where(picked == line, 1.0, 0.0).astype(BF16)
    mixed_ref[...] = dot(one_hot, out_ref[...]).astype(BF16)
    grad_ref[...] = dot(one_hot, back_ref[...]).astype(BF16)


def local(tokens, selections, router, w_gate, w_up, w_down, cotangent):
    devices = lax.axis_size("dp")
    experts = lax.axis_size("expert")
    chips = devices // 2
    slots = selections.shape[3]
    taken = experts * slots
    held, width = tokens.shape
    rows, half = w_gate.shape[1:]
    down_rows = w_down.shape[1]
    block = max(128, 2 * rows)
    hidden_block = max(128, 2 * down_rows)

    flat = selections.reshape(taken)
    x_sent = tokens.at[flat].get(mode="promise_in_bounds")
    d_sent = cotangent.at[flat].get(mode="promise_in_bounds")
    held_weights = lax.optimization_barrier((w_gate, w_up, w_down, x_sent))
    x_sent = held_weights[3]
    held_part = call(pack_weights, shape(rows + down_rows, width, BF16), held_weights[:3])
    parts = [None] * devices
    parts[0] = held_part
    for k in range(1, chips):
        parts[2 * k] = swap(held_part, "dp", 2 * k)
    for k in range(chips):
        parts[2 * k + 1] = swap(parts[2 * k], "dp", 1)

    sent = call(
        join,
        jax.ShapeDtypeStruct((experts, 2 * slots, width), BF16),
        (x_sent, d_sent),
    )
    got = [lax.all_to_all(sent, "expert", 0, 0, tiled=True)]
    x_rows, d_rows, *mids = call(
        functools.partial(prepare, slots, experts, chips, block),
        (shape(taken, width, BF16),) * 2 + (shape(taken, width + block, BF16),) * chips,
        (router, *got),
    )
    mids = [mids[0]] + [swap(mids[k], "dp", 2 * k) for k in range(1, chips)]

    lines = taken * hidden_block // width
    late_rows = taken + -(-(lines + 2) // 16) * 16
    outs = call(
        functools.partial(hidden_part, slots, experts, chips, hidden_block),
        (shape(late_rows, width, BF16),) * chips
        + (
            shape(taken, half, BF16),
            shape(taken, 128, F32),
            shape(width, half, BF16),
            shape(width, half, BF16),
            shape(half, width, BF16),
        ),
        (x_rows, d_rows, router, *parts),
        limit=16 if taken <= 64 else 40,
    )
    lates = list(outs[:chips])
    returned = call(
        functools.partial(row_part, slots),
        (shape(2 * slots, width, BF16),) * experts,
        (x_rows, router, lates[0], *outs[chips:]),
        limit=16 if taken <= 64 else 40,
    )
    own_late = lates[0]
    returned = [returned[0]] + [swap(returned[k], "expert", k) for k in range(experts - 1, 0, -1)][::-1]
    mixed, grad_tokens = call(
        functools.partial(combine, slots),
        (shape(held, width, BF16),) * 2,
        (selections[0, 0], *returned[::-1]),
        [pltpu.VMEM((taken, width), BF16)] * 2,
    )
    lates = [lates[0]] + [swap(lates[k], "dp", 2 * k) for k in range(1, chips)]
    mids = after(mids, returned[1])
    mids = mids + [swap(m, "dp", 1) for m in mids]
    near = after(lates[:-1], *returned)
    far = after(lates[-1:], mixed)
    lates = lates + [swap(t, "dp", 1) for t in near + far]
    grad_gate, grad_up, grad_down, grad_router = call(
        functools.partial(weight_grads, chips, block, hidden_block),
        (
            jax.ShapeDtypeStruct(w_gate.shape, F32),
            jax.ShapeDtypeStruct(w_up.shape, F32),
            jax.ShapeDtypeStruct(w_down.shape, F32),
            jax.ShapeDtypeStruct(router.shape, F32),
        ),
        (*mids, *lates),
        [pltpu.VMEM((block, 2 * half), F32), pltpu.VMEM((hidden_block, width), F32)],
        limit=16 if taken <= 64 else 40,
    )
    return mixed, grad_tokens, grad_gate, grad_up, grad_down, grad_router


def solution(mesh):
    return jax.shard_map(
        local,
        mesh=mesh,
        in_specs=(
            P(("dp", "expert"), None),
            P("dp", "expert", None, None),
            P("expert", None),
            P("expert", "dp", None),
            P("expert", "dp", None),
            P("expert", "dp", None),
            P(("dp", "expert"), None),
        ),
        out_specs=(
            P(("dp", "expert"), None),
            P(("dp", "expert"), None),
            P("expert", "dp", None),
            P("expert", "dp", None),
            P("expert", "dp", None),
            P("expert", None),
        ),
        check_vma=False,
    )
```

```python
import functools

import jax
import jax.numpy as jnp
from jax import lax
from jax.experimental import pallas as pl
from jax.experimental.pallas import tpu as pltpu
from jax.sharding import PartitionSpec as P

BF16 = jnp.bfloat16
F32 = jnp.float32
VMEM = pl.BlockSpec(memory_space=pltpu.VMEM)


def dot(left, right):
    return jnp.dot(left, right, preferred_element_type=F32)


def dot_rows(left, right):
    return lax.dot_general(left, right, (((0,), (0,)), ((), ())), preferred_element_type=F32)


def dot_cols(left, right):
    return lax.dot_general(left, right, (((1,), (1,)), ((), ())), preferred_element_type=F32)


def swap(value, axis, step):
    size = lax.axis_size(axis)
    return lax.ppermute(value, axis, [(i, i ^ step) for i in range(size)])


def after(values, *others):
    return list(lax.optimization_barrier((*values, *others))[: len(values)])


def shape(rows, columns, kind):
    return jax.ShapeDtypeStruct((rows, columns), kind)


def call(body, out_shape, args, scratch=(), flops=0, moved=0, limit=16):
    return pl.pallas_call(
        body,
        out_shape=out_shape,
        in_specs=[VMEM] * len(args),
        out_specs=jax.tree.map(lambda _: VMEM, out_shape),
        scratch_shapes=list(scratch),
        compiler_params=pltpu.CompilerParams(vmem_limit_bytes=limit << 20),
        cost_estimate=pl.CostEstimate(flops=flops, bytes_accessed=moved, transcendentals=0),
    )(*args)


def pack_weights(gate_ref, up_ref, down_ref, out_ref):
    rows, half = gate_ref.shape[1:]
    out_ref[:rows, :half] = gate_ref[0]
    out_ref[:rows, half:] = up_ref[0]
    out_ref[rows:, :] = down_ref[0]


def join(x_ref, d_ref, sent_ref):
    experts = sent_ref.shape[0]
    slots = x_ref.shape[0] // experts
    for e in range(experts):
        sent_ref[e, :slots, :] = x_ref[e * slots : (e + 1) * slots, :]
        sent_ref[e, slots:, :] = d_ref[e * slots : (e + 1) * slots, :]


def gate_of(x_ref, router_ref):
    logit = jnp.sum(
        x_ref[...].astype(F32) * router_ref[...].astype(F32), axis=1, keepdims=True
    )
    return jax.nn.sigmoid(logit)


def prepare(slots, chips, block, got_ref, router_ref, x_ref, d_ref, mid_ref):
    here = lax.axis_index("expert")
    for k in range(got_ref.shape[0]):
        x_ref[k * slots : (k + 1) * slots, :] = got_ref[here ^ k, :slots, :]
        d_ref[k * slots : (k + 1) * slots, :] = got_ref[here ^ k, slots:, :]
    gate_val = gate_of(x_ref, router_ref)
    back = (gate_val * d_ref[...].astype(F32)).astype(BF16)
    fill_mid(mid_ref, back, x_ref, chips, chips - 1, block)


def fill_mid(ref, back, x_ref, chips, k, block):
    tall, width = back.shape
    each = tall * block // width
    ref[:tall, :] = back
    mine = lax.axis_index("dp") // 2
    start = ((mine ^ k) * (width // chips)) // block * block
    cut = x_ref[:, pl.ds(pl.multiple_of(start, 128), block)]
    ref[tall : tall + each, :] = lines_of(cut, each)


def lines_of(value, rows):
    count = value.shape[0] // rows
    return jnp.concatenate([value[i * rows : (i + 1) * rows, :] for i in range(count)], axis=1)


def rows_of(lines, columns):
    count = lines.shape[1] // columns
    return [lines[:, i * columns : (i + 1) * columns] for i in range(count)]


def hidden_part(slots, experts, chips, block, hidden_block, *refs):
    devices = 2 * chips
    x_ref, d_ref, router_ref = refs[:3]
    parts = refs[3 : 3 + devices]
    outs = refs[3 + devices :]
    late_refs = outs[:chips]
    hidden_ref, logit_ref, gate_ref, gate_w, up_w, down_w = outs[chips:]
    width, half = gate_w.shape
    rows = width // devices
    down_rows = half // devices
    me = lax.axis_index("dp")
    for r in range(devices):
        at = pl.ds(pl.multiple_of((me ^ r) * rows, rows), rows)
        gate_w[at, :] = parts[r][:rows, :half]
        up_w[at, :] = parts[r][:rows, half:]
        at = pl.ds(pl.multiple_of((me ^ r) * down_rows, down_rows), down_rows)
        down_w[at, :] = parts[r][rows:, :]
    x = x_ref[...]
    d = d_ref[...]
    tall = x.shape[0]
    gate_val = gate_of(x_ref, router_ref)
    act_gate = dot(x, gate_w[...])
    act_up = dot(x, up_w[...])
    sigma = jax.nn.sigmoid(act_gate)
    silu = act_gate * sigma
    hidden = (silu * act_up).astype(BF16)
    hidden_ref[...] = hidden
    raw = dot_cols(d, down_w[...])
    gate_grad = jnp.sum(hidden.astype(F32) * raw, axis=1, keepdims=True)
    logit_grad = gate_grad * gate_val * (1.0 - gate_val)
    hidden_grad = gate_val * raw
    grad_gate = (hidden_grad * act_up * sigma * (1.0 + act_gate * (1.0 - sigma))).astype(BF16)
    grad_up = (hidden_grad * silu).astype(BF16)
    logit_ref[...] = jnp.broadcast_to(logit_grad, logit_ref.shape)
    gate_ref[...] = jnp.broadcast_to(gate_val, gate_ref.shape)
    back = (gate_val * d.astype(F32)).astype(BF16)
    term = jnp.sum(logit_grad * x.astype(F32), axis=0, keepdims=True)
    high = term.astype(BF16).astype(F32)
    low = term - high
    mine = me // 2
    hidden_each = tall * hidden_block // width
    tail = late_refs[-1].shape[0] - tall
    empty = jnp.zeros((tail - hidden_each - 2, width), F32)
    for k, ref in enumerate(late_refs):
        at = ref.shape[0] - tail - tall
        if at:
            fill_mid(ref, back, x_ref, chips, k, block)
        ref[at : at + tall, :half] = grad_gate
        ref[at : at + tall, half:] = grad_up
        start = ((mine ^ k) * (half // chips)) // hidden_block * hidden_block
        cut = hidden_ref[:, pl.ds(pl.multiple_of(start, 128), hidden_block)].astype(F32)
        lines = lines_of(cut, hidden_each)
        ref[at + tall :, :] = jnp.concatenate([lines, high, low, empty], axis=0).astype(BF16)


def row_part(slots, router_ref, late_ref, hidden_ref, logit_ref, gate_ref, gate_w, up_w, down_w, *outs):
    tall, half = hidden_ref.shape
    out_rows = (gate_ref[:, :1] * dot(hidden_ref[...], down_w[...])).astype(BF16)
    row_grads = dot_cols(late_ref[:tall, :half], gate_w[...])
    row_grads = row_grads + dot_cols(late_ref[:tall, half:], up_w[...])
    row_grads = (row_grads + logit_ref[:, :1] * router_ref[...].astype(F32)).astype(BF16)
    for k, ref in enumerate(outs):
        ref[:slots, :] = out_rows[k * slots : (k + 1) * slots, :]
        ref[slots:, :] = row_grads[k * slots : (k + 1) * slots, :]


def weight_grads(tall, chips, block, hidden_block, *refs):
    devices = 2 * chips
    pairs, rest = [], list(refs)
    for i in range(devices):
        first = rest.pop(0)
        pairs.append((first, rest.pop(0) if i % chips == chips - 1 else first))
    gate_ref, up_ref, down_ref, router_ref, sum_ref, down_sum_ref = rest
    width = router_ref.shape[1]
    half = gate_ref.shape[2]
    scale = 1.0 / devices
    each = tall * block // width
    hidden_each = tall * hidden_block // width
    me = lax.axis_index("dp")
    total = None
    count = devices if devices * tall <= 1024 else chips
    for c in range(devices // count):
        mids = [m for m, _ in pairs[c * count : (c + 1) * count]]
        lates = [(t, tall + each if m is t else 0) for m, t in pairs[c * count : (c + 1) * count]]
        backs = jnp.concatenate([m[:tall, :] for m in mids], axis=0)
        feats = jnp.concatenate(
            [p for m in mids for p in rows_of(m[tall : tall + each, :], block)], axis=0
        )
        grads = jnp.concatenate([t[at : at + tall, :] for t, at in lates], axis=0)
        term = dot_rows(feats, grads)
        sum_ref[...] = term if c == 0 else sum_ref[...] + term
        tails = [t[at + tall :, :].astype(F32) for t, at in lates]
        hidden = jnp.concatenate(
            [p for t in tails for p in rows_of(t[:hidden_each, :], hidden_block)], axis=0
        ).astype(BF16)
        term = dot_rows(hidden, backs)
        down_sum_ref[...] = term if c == 0 else down_sum_ref[...] + term
        for t in tails:
            total = t if total is None else total + t
    rows = gate_ref.shape[1]
    at = pl.ds(pl.multiple_of((me * rows) % block, rows), rows)
    gate_ref[0] = sum_ref[at, :half] * scale
    up_ref[0] = sum_ref[at, half:] * scale
    rows = down_ref.shape[1]
    at = pl.ds(pl.multiple_of((me * rows) % hidden_block, rows), rows)
    down_ref[0] = down_sum_ref[at, :] * scale
    line = total[hidden_each : hidden_each + 1, :] + total[hidden_each + 1 : hidden_each + 2, :]
    router_ref[...] = line * scale


def combine(slots, chosen_ref, *refs):
    got, (mixed_ref, grad_ref, out_ref, back_ref) = refs[:-4], refs[-4:]
    me = lax.axis_index("expert")
    for k, ref in enumerate(got[::-1]):
        at = pl.ds(pl.multiple_of((me ^ k) * slots, slots), slots)
        out_ref[at, :] = ref[:slots, :]
        back_ref[at, :] = ref[slots:, :]
    chosen = chosen_ref[...]
    line = jnp.concatenate([chosen[e : e + 1, :] for e in range(len(got))], axis=1)
    picked = lax.broadcasted_iota(jnp.int32, (mixed_ref.shape[0], line.shape[1]), 0)
    one_hot = jnp.where(picked == line, 1.0, 0.0).astype(BF16)
    mixed_ref[...] = dot(one_hot, out_ref[...]).astype(BF16)
    grad_ref[...] = dot(one_hot, back_ref[...]).astype(BF16)


def local(tokens, selections, router, w_gate, w_up, w_down, cotangent):
    devices = lax.axis_size("dp")
    experts = lax.axis_size("expert")
    chips = devices // 2
    slots = selections.shape[3]
    taken = experts * slots
    held, width = tokens.shape
    rows, half = w_gate.shape[1:]
    down_rows = w_down.shape[1]
    block = max(128, 2 * rows)
    hidden_block = max(128, 2 * down_rows)

    flat = selections.reshape(taken)
    x_sent = tokens.at[flat].get(mode="promise_in_bounds")
    d_sent = cotangent.at[flat].get(mode="promise_in_bounds")
    held_weights = lax.optimization_barrier((w_gate, w_up, w_down, x_sent))
    x_sent = held_weights[3]
    held_part = call(pack_weights, shape(rows + down_rows, width, BF16), held_weights[:3])
    parts = [None] * devices
    parts[0] = held_part
    for k in range(1, chips):
        parts[2 * k] = swap(held_part, "dp", 2 * k)
    for k in range(chips):
        parts[2 * k + 1] = swap(parts[2 * k], "dp", 1)

    sent = call(
        join,
        jax.ShapeDtypeStruct((experts, 2 * slots, width), BF16),
        (x_sent, d_sent),
    )
    got = lax.all_to_all(sent, "expert", 0, 0, tiled=True)
    mid_rows = taken + taken * block // width
    late_rows = taken + -(-(taken * hidden_block // width + 2) // 16) * 16
    x_rows, d_rows, far_mid = call(
        functools.partial(prepare, slots, chips, block),
        (shape(taken, width, BF16),) * 2 + (shape(mid_rows, width, BF16),),
        (got, router),
    )
    far_mid = swap(far_mid, "dp", devices - 2)
    outs = call(
        functools.partial(hidden_part, slots, experts, chips, block, hidden_block),
        (shape(mid_rows + late_rows, width, BF16),) * (chips - 1)
        + (shape(late_rows, width, BF16),)
        + (
            shape(taken, half, BF16),
            shape(taken, 128, F32),
            shape(taken, 128, F32),
            shape(width, half, BF16),
            shape(width, half, BF16),
            shape(half, width, BF16),
        ),
        (x_rows, d_rows, router, *parts),
        limit=16 if taken <= 64 else 40,
    )
    lates = list(outs[:chips])
    returned = call(
        functools.partial(row_part, slots),
        (shape(2 * slots, width, BF16),) * experts,
        (router, lates[-1], *outs[chips:]),
        limit=16 if taken <= 64 else 40,
    )
    other_mid = swap(far_mid, "dp", 1)
    returned = list(returned)
    returned[-1] = after(returned[-1:], other_mid)[0]
    returned = [returned[0]] + [swap(returned[k], "expert", k) for k in range(experts - 1, 0, -1)][::-1]
    mixed, grad_tokens = call(
        functools.partial(combine, slots),
        (shape(held, width, BF16),) * 2,
        (selections[0, 0], *returned[::-1]),
        [pltpu.VMEM((taken, width), BF16)] * 2,
    )
    lates = [lates[0]] + [swap(lates[k], "dp", 2 * k) for k in range(1, chips)]
    own_late = swap(lates[0], "dp", 1)
    lates = after(lates[:-1], *returned) + after(lates[-1:], mixed)
    others = [own_late] + [swap(t, "dp", 1) for t in lates[1:]]
    lates = lates[:-1] + [far_mid, lates[-1]] + others[:-1] + [other_mid, others[-1]]
    grad_gate, grad_up, grad_down, grad_router = call(
        functools.partial(weight_grads, taken, chips, block, hidden_block),
        (
            jax.ShapeDtypeStruct(w_gate.shape, F32),
            jax.ShapeDtypeStruct(w_up.shape, F32),
            jax.ShapeDtypeStruct(w_down.shape, F32),
            jax.ShapeDtypeStruct(router.shape, F32),
        ),
        (*lates,),
        [pltpu.VMEM((block, 2 * half), F32), pltpu.VMEM((hidden_block, width), F32)],
        limit=16 if taken <= 64 else 40,
    )
    return mixed, grad_tokens, grad_gate, grad_up, grad_down, grad_router


def solution(mesh):
    return jax.shard_map(
        local,
        mesh=mesh,
        in_specs=(
            P(("dp", "expert"), None),
            P("dp", "expert", None, None),
            P("expert", None),
            P("expert", "dp", None),
            P("expert", "dp", None),
            P("expert", "dp", None),
            P(("dp", "expert"), None),
        ),
        out_specs=(
            P(("dp", "expert"), None),
            P(("dp", "expert"), None),
            P("expert", "dp", None),
            P("expert", "dp", None),
            P("expert", "dp", None),
            P("expert", None),
        ),
        check_vma=False,
    )
```
